32 devices in a mesh: branch: 4 (over z), ctx: 8 (over y, x, core).
Axes of the slice: x: 2, y: 2, z: 4, core: 2. Of those that a mesh axis runs over, the one named last changes fastest.
Arguments:
- summary_q: bfloat16 [16384, 2560], P(('branch', 'ctx')), may hold values from -32 to 32
- summary_kv: bfloat16 [16384, 2, 512], P(('branch', 'ctx')), may hold values from -12 to 12
- kv_cache: bfloat16 [128, 2, 128, 512], P(('branch', 'ctx')), may hold values from -9 to 9
- block_slot: int32 [128], replicated, may hold values from 0 to 127, as said below
- tile_blocks: int32 [128, 4], P(('branch', 'ctx')), may hold values from 0 to 127, as said below
- tile_count: int32 [128], P(('branch', 'ctx')), may hold values from 2 to 4
Outputs:
- attended: bfloat16 [16384, 2560], P(('branch', 'ctx'))
The draws below stay inside these ranges and needn't reach their ends.
Inputs may be any that keep to these rules, and one draw needn't show every extreme that they name: `block_slot`: each slot number appears once; slot s lies on the device of index s // 4 along branch+ctx. `tile_blocks`: among the first tile_count[t] entries of the 4 tiles of one device, at most 2 are stored on devices of one ctx index and at most 1 on one device; entries after tile_count[t] are not read.
All inputs are finite; a program needn't handle non-finite values.
Results may differ from the reference program's by a relative error of at most 0.0045.
Values may be sent and summed in bfloat16 or wider, within the bound.
A program may use at most 192 MiB of HBM per device.

```python
import jax
import jax.numpy as jnp
from jax import lax

HEAD = 128
KVH = 4
REP = 5
BLOCK = 128
TILE = 128
TILES_DEV = 4
REQ_TILES = 32
BLK_DEV = 4
GROUPS = 4
SHARDS = 8
DEVS = 32
QW = 2560
KVW = 512
LIST = 4
CAPB = 2
TILES = 128
TOKENS = 16384
BLOCKS = 128


def plan_lists(key):
    base_key = jax.random.fold_in(key, 1013)
    subkeys = jax.random.split(base_key, 11)
    block_slot = jax.random.permutation(subkeys[0], BLOCKS).astype(jnp.int32)
    block_of_slot = jnp.argsort(block_slot).astype(jnp.int32)
    per_dev = TILES_DEV * LIST
    hot_col = jax.random.randint(subkeys[1], (), 0, SHARDS)
    hot_row = jax.random.randint(subkeys[2], (), 0, GROUPS)
    hot_tile = jax.random.randint(subkeys[3], (DEVS, 1), 0, TILES_DEV)
    positions = jnp.arange(per_dev, dtype=jnp.int32)[None, :]
    tile_of = positions // LIST
    within = positions % LIST
    is_hot = (tile_of == hot_tile) & (within < CAPB)
    rest_rank = jnp.cumsum(jnp.where(is_hot, 0, 1), axis=1) - 1
    rest_rank = jnp.maximum(rest_rank, 0)
    group_count = (per_dev - CAPB + CAPB - 1) // CAPB
    offset = jax.random.randint(subkeys[4], (DEVS, 1), 0, SHARDS - group_count)
    group_of = rest_rank // CAPB
    member = rest_rank % CAPB
    column = jnp.where(is_hot, hot_col, (hot_col + 1 + offset + group_of) % SHARDS)
    row_start = jax.random.randint(subkeys[5], (DEVS, per_dev), 0, GROUPS)
    start_row = jnp.take_along_axis(row_start, group_of, axis=1)
    row_of = jnp.where(is_hot, (hot_row + within) % GROUPS, (start_row + member) % GROUPS)
    local_slot = jax.random.randint(subkeys[6], (DEVS, per_dev), 0, BLK_DEV)
    stored = (row_of * SHARDS + column) * BLK_DEV + local_slot
    tile_blocks = block_of_slot[stored].reshape(TILES, LIST).astype(jnp.int32)
    heavy_dev = jax.random.randint(subkeys[7], (DEVS, 1), 0, 4) == 0
    light_count = jax.random.randint(subkeys[8], (DEVS, TILES_DEV), max(CAPB, LIST // 2), LIST + 1)
    counts = jnp.where(heavy_dev, LIST, light_count).reshape(TILES)
    full_tile = jax.random.randint(subkeys[9], (), 0, TILES)
    low_tile = (full_tile + 1 + jax.random.randint(subkeys[10], (), 0, TILES - 1)) % TILES
    counts = counts.at[full_tile].set(LIST).at[low_tile].set(CAPB)
    return (block_slot, tile_blocks, counts.astype(jnp.int32))


def draw_summary_q(key, part):
    bulk_key = jax.random.fold_in(key, 31)
    drawn = jax.random.truncated_normal(bulk_key, -6.0, 6.0, (TOKENS, QW), jnp.float32)
    return drawn.astype(jnp.bfloat16)


def draw_summary_kv(key, part):
    bulk_key = jax.random.fold_in(key, 47)
    drawn = 2.0 * jax.random.truncated_normal(bulk_key, -6.0, 6.0, (TOKENS, 2, KVW), jnp.float32)
    return drawn.astype(jnp.bfloat16)


def draw_block_slot(key, part):
    return plan_lists(key)[0]


def draw_tile_blocks(key, part):
    return plan_lists(key)[1]


def draw_tile_count(key, part):
    return plan_lists(key)[2]


def block_levels(rng, shape, shards, smallest, largest):
    factor_of, own = 1.0, jax.random.fold_in(rng, 6)
    for dim, parts in shards:
        steps = jnp.exp(jax.random.uniform(jax.random.fold_in(own, dim), (parts,), jnp.float32, smallest / len(shards), largest / len(shards)))
        factor_of = factor_of * jnp.repeat(steps, shape[dim] // parts).reshape([-1 if axis == dim else 1 for axis in range(len(shape))])
    return factor_of


def normal_values(key, shape, width, most, pieces=(), held_as=jnp.bfloat16):
    values = jax.random.normal(key, shape, jnp.float32) * width
    if len(pieces) > 0:
        values = block_levels(key, shape, pieces, -0.22, 0.18) * values
    return jnp.clip(values, min=-most, max=most).astype(held_as)


def setup_inputs(seed: int = 0) -> dict:
    seeds = jax.random.split(jax.random.key(seed), 7)
    return {
        "summary_q": draw_summary_q(jax.random.fold_in(seeds[6], 71), 0),
        "summary_kv": draw_summary_kv(jax.random.fold_in(seeds[6], 71), 0),
        "kv_cache": normal_values(seeds[2], (BLOCKS, 2, BLOCK, KVW), 1.5, 9.0, ((0, 32),)),
        "block_slot": draw_block_slot(jax.random.fold_in(seeds[6], 71), 0),
        "tile_blocks": draw_tile_blocks(jax.random.fold_in(seeds[6], 71), 0),
        "tile_count": draw_tile_count(jax.random.fold_in(seeds[6], 71), 0),
    }


def reference(summary_q, summary_kv, kv_cache, block_slot, tile_blocks, tile_count):
    tile_num = tile_blocks.shape[0]
    list_len = tile_blocks.shape[1]
    span_len = REQ_TILES * TILE
    queries = summary_q.reshape(tile_num, TILE, KVH, REP, HEAD)
    rolled_kv = jnp.roll(summary_kv, -TILES_DEV * TILE, axis=0)
    request_kv = rolled_kv.reshape(tile_num // REQ_TILES, span_len, 2, KVH, HEAD)
    tile_ids = jnp.arange(tile_num, dtype=jnp.int32)
    key_pos = jnp.arange(span_len, dtype=jnp.int32)
    score_scale = HEAD ** -0.5

    def one_tile(packed):
        query_tile, listed, count_live, tile_id = packed
        moved_id = (tile_id - TILES_DEV + tile_num) % tile_num
        span_kv = request_kv[moved_id // REQ_TILES]
        query_pos = (moved_id % REQ_TILES) * TILE + jnp.arange(TILE, dtype=jnp.int32)
        summary_mask = key_pos[None, :] <= query_pos[:, None]
        stored_at = block_slot[listed]
        fetched = kv_cache[stored_at]
        branch_keys = fetched[:, 0].reshape(list_len * BLOCK, KVH, HEAD)
        branch_values = fetched[:, 1].reshape(list_len * BLOCK, KVH, HEAD)
        key_rows = jnp.concatenate([span_kv[:, 0], branch_keys], axis=0).astype(jnp.float32)
        value_rows = jnp.concatenate([span_kv[:, 1], branch_values], axis=0).astype(jnp.float32)
        live_block = jnp.arange(list_len, dtype=jnp.int32) < count_live
        live_keys = jnp.repeat(live_block, BLOCK)
        key_mask = jnp.concatenate([summary_mask, jnp.broadcast_to(live_keys[None, :], (TILE, list_len * BLOCK))], axis=1)
        scores = jnp.einsum("qgrd,kgd->grqk", query_tile.astype(jnp.float32), key_rows) * score_scale
        scores = jnp.where(key_mask[None, None], scores, -jnp.inf)
        row_max = jnp.max(scores, axis=-1, keepdims=True)
        weights = jnp.exp(scores - row_max)
        row_sum = jnp.sum(weights, axis=-1)
        rounded = lax.optimization_barrier(weights.astype(jnp.bfloat16)).astype(jnp.float32)
        attended = jnp.einsum("grqk,kgd->qgrd", rounded, value_rows) / jnp.transpose(row_sum, (2, 0, 1))[..., None]
        return attended.reshape(TILE, KVH * REP * HEAD).astype(jnp.bfloat16)

    result = lax.map(one_tile, (queries, tile_blocks, tile_count, tile_ids))
    return result.reshape(tile_num * TILE, KVH * REP * HEAD)
```

```python
import functools
import math

import jax
import jax.numpy as jnp
from jax import lax
from jax.experimental import pallas as pl
from jax.experimental.pallas import tpu as pltpu
from jax.sharding import PartitionSpec as P

HEAD = 128
REQ_TILES = 32
CHUNK = 4
SCALE = math.log2(math.e) * HEAD**-0.5


def from_behind(value, axis, steps):
    count = lax.axis_size(axis)
    pairs = [(source, (source + steps) % count) for source in range(count)]
    return lax.ppermute(value, axis, pairs)


def request_table(dest_index, live_mask, count_dest, capacity, payload):
    onehot = (
        (dest_index[:, None] == jnp.arange(count_dest, dtype=jnp.int32)[None, :])
        & live_mask[:, None]
    ).astype(jnp.int32)
    rank_within = jnp.sum(onehot * (jnp.cumsum(onehot, axis=0) - 1), axis=1)
    position = dest_index * capacity + rank_within
    target = jnp.where(live_mask, position, -1)
    slot_ids = jnp.arange(count_dest * capacity, dtype=jnp.int32)
    requests = jnp.max(
        jnp.where(target[:, None] == slot_ids[None, :], payload[:, None], -1), axis=0
    )
    return (requests.reshape(count_dest, capacity), position)


def absorb(index, key_rows, value_rows, mask, first, qs, top, acc):
    scores = lax.dot_general(
        qs[index], key_rows, (((1,), (1,)), ((), ())), preferred_element_type=jnp.float32
    )
    if mask is not None:
        scores = jnp.where(mask, scores, -jnp.inf)
    block_max = jnp.max(scores, axis=1, keepdims=True)
    ones = jnp.ones_like(value_rows)
    values = jnp.concatenate([value_rows, ones], axis=1)
    if first:
        new_max = jnp.broadcast_to(block_max, top.shape[1:])
        weights = jnp.exp2((scores - block_max) * SCALE).astype(jnp.bfloat16)
        acc[index] = jnp.dot(weights, values, preferred_element_type=jnp.float32)
    else:
        old_max = top[index]
        new_max = jnp.maximum(old_max, block_max)
        wide = jnp.concatenate([new_max] * (scores.shape[1] // HEAD), axis=1)
        weights = jnp.exp2((scores - wide) * SCALE).astype(jnp.bfloat16)
        rescale = jnp.exp2((old_max - new_max) * SCALE)
        acc[index] = acc[index] * jnp.concatenate([rescale, rescale], axis=1) + jnp.dot(
            weights, values, preferred_element_type=jnp.float32
        )
    top[index] = new_max


def head_lanes(group):
    return pl.ds(pl.multiple_of(group * HEAD, HEAD), HEAD)


def own_block(own, tile_num, groups, qs, top, acc):
    tile_rows = own.shape[0] // tile_num
    repeat = qs.shape[1] // tile_rows
    shape = (repeat * tile_rows, own.shape[0])
    query_row = lax.rem(lax.broadcasted_iota(jnp.int32, shape, 0), tile_rows)
    key_row = lax.broadcasted_iota(jnp.int32, shape, 1)

    def body(index, carry):
        group, tile = lax.div(index, tile_num), lax.rem(index, tile_num)
        lanes = head_lanes(group)
        keys = own[:, lanes]
        values = own[:, pl.ds(pl.multiple_of((groups + group) * HEAD, HEAD), HEAD)]
        mask = key_row <= query_row + tile * tile_rows
        absorb(index, keys, values, mask, True, qs, top, acc)
        return carry

    lax.fori_loop(0, groups * tile_num, body, 0)


def earlier_block(block, tile_num, groups, qs, top, acc):
    def body(group, carry):
        keys = block[:, head_lanes(group)]
        values = block[:, pl.ds(pl.multiple_of((groups + group) * HEAD, HEAD), HEAD)]
        for tile in range(tile_num):
            absorb(group * tile_num + tile, keys, values, None, False, qs, top, acc)
        return carry

    lax.fori_loop(0, groups, body, 0)


def branch_blocks(position, count, received, tile_num, list_len, groups, qs, top, acc):
    block_len = received.shape[2]
    shape = (qs.shape[1], CHUNK * block_len)
    key_block = lax.div(lax.broadcasted_iota(jnp.int32, shape, 1), block_len)

    def body(index, carry):
        group, tile = lax.div(index, tile_num), lax.rem(index, tile_num)
        lanes = head_lanes(group)
        for start in range(0, list_len, CHUNK):
            where = [position[tile * list_len + start + i] for i in range(CHUNK)]
            keys = jnp.concatenate([received[w, 0, :, lanes] for w in where], axis=0)
            values = jnp.concatenate([received[w, 1, :, lanes] for w in where], axis=0)
            mask = key_block < count[tile] - start
            absorb(index, keys, values, mask, False, qs, top, acc)
        return carry

    lax.fori_loop(0, groups * tile_num, body, 0)


def load_queries(q_ref, tile_num, groups, qs):
    tile_rows = q_ref.shape[0] // tile_num
    repeat = qs.shape[1] // tile_rows
    for group in range(groups):
        for tile in range(tile_num):
            for r in range(repeat):
                head = group * repeat + r
                qs[group * tile_num + tile, r * tile_rows : (r + 1) * tile_rows, :] = q_ref[
                    tile * tile_rows : (tile + 1) * tile_rows, head * HEAD : (head + 1) * HEAD
                ]


def store_result(o_ref, tile_num, groups, acc):
    tile_rows = o_ref.shape[0] // tile_num
    repeat = acc.shape[1] // tile_rows
    for group in range(groups):
        for tile in range(tile_num):
            for r in range(repeat):
                head = group * repeat + r
                part = acc[group * tile_num + tile, r * tile_rows : (r + 1) * tile_rows, :]
                o_ref[
                    tile * tile_rows : (tile + 1) * tile_rows, head * HEAD : (head + 1) * HEAD
                ] = (part[:, :HEAD] / part[:, HEAD:]).astype(o_ref.dtype)


def attend(tile_num, list_len, groups, position, count, place, q_ref, own, earlier, received, o_ref, qs, top, acc):
    load_queries(q_ref, tile_num, groups, qs)
    own_block(own, tile_num, groups, qs, top, acc)

    def body(step, carry):
        earlier_block(earlier.at[step], tile_num, groups, qs, top, acc)
        return carry

    lax.fori_loop(0, place[0], body, 0)
    branch_blocks(position, count, received, tile_num, list_len, groups, qs, top, acc)
    store_result(o_ref, tile_num, groups, acc)


def local(summary_q, summary_kv, kv_cache, block_slot, tile_blocks, tile_count):
    shards = lax.axis_size("ctx")
    tile_num, list_len = tile_blocks.shape
    blk_dev = kv_cache.shape[0]
    block_len = kv_cache.shape[2]
    kv_width = kv_cache.shape[3]
    groups = kv_width // HEAD
    rows = summary_q.shape[0]
    tile_rows = rows // tile_num
    repeat = summary_q.shape[1] // kv_width
    col_cap = max(2, -(-(tile_num * list_len) // shards))
    req_devs = REQ_TILES // tile_num
    entries = tile_blocks.reshape(-1)
    live_mask = (jnp.arange(list_len, dtype=jnp.int32)[None, :] < tile_count[:, None]).reshape(-1)
    block_ids = jnp.arange(block_slot.shape[0], dtype=jnp.int32)
    stored_at = jnp.sum(
        jnp.where(entries[:, None] == block_ids[None, :], block_slot[None, :], 0), axis=1
    )
    owner_dev = stored_at // blk_dev
    local_slot = stored_at % blk_dev
    column = lax.all_gather(kv_cache, "branch", axis=0, tiled=True)
    requests, position = request_table(
        owner_dev % shards, live_mask, shards, col_cap, owner_dev // shards * blk_dev + local_slot
    )
    payload = column[
        jnp.maximum(lax.all_to_all(requests, "ctx", split_axis=0, concat_axis=0, tiled=True), 0)
    ]
    received = lax.all_to_all(payload, "ctx", split_axis=0, concat_axis=0, tiled=True)
    received = received.reshape(-1, 2, block_len, kv_width)
    position = jnp.where(live_mask, position, 0)
    flat_index = lax.axis_index("branch") * shards + lax.axis_index("ctx")
    place = (flat_index - 1 + req_devs) % req_devs
    own = summary_kv.reshape(rows, 2 * kv_width)
    passed = own
    earlier = []
    for _ in range(1, req_devs):
        passed = from_behind(passed, ("branch", "ctx"), 1)
        earlier.append(passed)
    vmem, smem = pl.BlockSpec(memory_space=pltpu.VMEM), pl.BlockSpec(memory_space=pltpu.SMEM)
    return pl.pallas_call(
        functools.partial(attend, tile_num, list_len, groups),
        out_shape=jax.ShapeDtypeStruct(summary_q.shape, jnp.bfloat16),
        in_specs=[smem] * 3 + [vmem] * 4,
        out_specs=vmem,
        scratch_shapes=[
            pltpu.VMEM((groups * tile_num, repeat * tile_rows, HEAD), jnp.bfloat16),
            pltpu.VMEM((groups * tile_num, repeat * tile_rows, HEAD), jnp.float32),
            pltpu.VMEM((groups * tile_num, repeat * tile_rows, 2 * HEAD), jnp.float32),
        ],
        compiler_params=pltpu.CompilerParams(vmem_limit_bytes=60 * 2**20),
    )(position, tile_count, place[None], summary_q, own, jnp.stack(earlier), received)


def solution(mesh):
    in_specs = (
        P(("branch", "ctx"), None),
        P(("branch", "ctx"), None, None),
        P(("branch", "ctx"), None, None, None),
        P(),
        P(("branch", "ctx"), None),
        P(("branch", "ctx")),
    )
    out_specs = P(("branch", "ctx"), None)
    return jax.shard_map(local, mesh=mesh, in_specs=in_specs, out_specs=out_specs, check_vma=False)
```

```python
import functools
import math

import jax
import jax.numpy as jnp
from jax import lax
from jax.experimental import pallas as pl
from jax.experimental.pallas import tpu as pltpu
from jax.sharding import PartitionSpec as P

HEAD = 128
REQ_TILES = 32
CHUNK = 4
HALVES = 2
STAGES = 7
SCALE = math.log2(math.e) * HEAD**-0.5


def request_table(dest_index, live_mask, count_dest, capacity, payload):
    onehot = (
        (dest_index[:, None] == jnp.arange(count_dest, dtype=jnp.int32)[None, :])
        & live_mask[:, None]
    ).astype(jnp.int32)
    rank_within = jnp.sum(onehot * (jnp.cumsum(onehot, axis=0) - 1), axis=1)
    position = dest_index * capacity + rank_within
    target = jnp.where(live_mask, position, -1)
    slot_ids = jnp.arange(count_dest * capacity, dtype=jnp.int32)
    requests = jnp.max(
        jnp.where(target[:, None] == slot_ids[None, :], payload[:, None], -1), axis=0
    )
    return (requests.reshape(count_dest, capacity), position)


def absorb(group, tile, key_rows, value_rows, mask, first, q_ref, top, acc):
    groups, tile_num = acc.shape[:2]
    tile_rows = q_ref.shape[0] // tile_num
    repeat = q_ref.shape[1] // (groups * HEAD)
    token = pl.ds(pl.multiple_of(tile * tile_rows, tile_rows), tile_rows)
    index = (group, tile)
    queries = jnp.concatenate(
        [q_ref[token, head_lanes(group * repeat + r)] for r in range(repeat)], axis=0
    )
    scores = lax.dot_general(
        queries, key_rows, (((1,), (1,)), ((), ())), preferred_element_type=jnp.float32
    )
    if mask is not None:
        scores = jnp.where(mask, scores, -jnp.inf)
    block_max = jnp.max(scores, axis=1, keepdims=True)
    ones = jnp.ones_like(value_rows)
    values = jnp.concatenate([value_rows, ones], axis=1)
    if first:
        new_max = jnp.broadcast_to(block_max, top.shape[2:])
        weights = jnp.exp2((scores - block_max) * SCALE).astype(jnp.bfloat16)
        acc[index] = jnp.dot(weights, values, preferred_element_type=jnp.float32)
    else:
        old_max = top[index]
        new_max = jnp.maximum(old_max, block_max)
        wide = jnp.concatenate([new_max] * (scores.shape[1] // HEAD), axis=1)
        weights = jnp.exp2((scores - wide) * SCALE).astype(jnp.bfloat16)
        rescale = jnp.exp2((old_max - new_max) * SCALE)
        acc[index] = acc[index] * jnp.concatenate([rescale, rescale], axis=1) + jnp.dot(
            weights, values, preferred_element_type=jnp.float32
        )
    top[index] = new_max


def head_lanes(group):
    return pl.ds(pl.multiple_of(group * HEAD, HEAD), HEAD)


def own_block(own, q_ref, top, acc):
    groups, tile_num = acc.shape[:2]
    tile_rows = own.shape[0] // tile_num
    shape = (acc.shape[2], own.shape[0])
    query_row = lax.rem(lax.broadcasted_iota(jnp.int32, shape, 0), tile_rows)
    key_row = lax.broadcasted_iota(jnp.int32, shape, 1)

    def body(group, carry):
        keys, values = own[:, head_lanes(group)], own[:, head_lanes(groups + group)]
        for tile in range(tile_num):
            mask = key_row <= query_row + tile * tile_rows
            absorb(group, tile, keys, values, mask, True, q_ref, top, acc)
        return carry

    lax.fori_loop(0, groups, body, 0)


def earlier_block(block, q_ref, top, acc):
    groups, tile_num = acc.shape[:2]

    def body(group, carry):
        keys, values = block[:, head_lanes(group)], block[:, head_lanes(groups + group)]
        for tile in range(tile_num):
            absorb(group, tile, keys, values, None, False, q_ref, top, acc)
        return carry

    lax.fori_loop(0, groups, body, 0)


def branch_blocks(half, position, count, received, q_ref, top, acc):
    groups, tile_num = acc.shape[:2]
    list_len = position.shape[0] // tile_num
    block_len = received.shape[2]
    shape = (acc.shape[2], CHUNK * block_len)
    key_block = lax.div(lax.broadcasted_iota(jnp.int32, shape, 1), block_len)

    def body(tile, carry):
        for start in range(0, list_len, CHUNK):
            where = [position[tile * list_len + start + i] for i in range(CHUNK)]
            mask = key_block < count[tile] - start
            for sub in range(groups // HALVES):
                lanes = slice(sub * HEAD, (sub + 1) * HEAD)
                keys = jnp.concatenate([received[w, 0, :, lanes] for w in where], axis=0)
                values = jnp.concatenate([received[w, 1, :, lanes] for w in where], axis=0)
                group = half * (groups // HALVES) + sub
                absorb(group, tile, keys, values, mask, False, q_ref, top, acc)
        return carry

    lax.fori_loop(0, tile_num, body, 0)


def store_result(o_ref, acc):
    groups, tile_num, stacked, _ = acc.shape
    tile_rows = o_ref.shape[0] // tile_num
    repeat = stacked // tile_rows

    def body(group, carry):
        for tile in range(tile_num):
            for r in range(repeat):
                part = acc[group, tile, r * tile_rows : (r + 1) * tile_rows, :]
                o_ref[
                    tile * tile_rows : (tile + 1) * tile_rows, head_lanes(group * repeat + r)
                ] = (part[:, :HEAD] / part[:, HEAD:]).astype(o_ref.dtype)
        return carry

    lax.fori_loop(0, groups, body, 0)


def join(
    planes, shards, capacity,
    wanted, position, count, q_ref, own, cache, o_ref,
    earlier, relay, column, payload, received, top, acc,
    kv_send, kv_recv, hop_sem, fwd_send, gather_send, gather_recv, list_send, list_recv,
):
    z, c = lax.axis_index("branch"), lax.axis_index("ctx")
    req_devs = earlier.shape[0] + 1
    place = lax.rem(c + req_devs - 1, req_devs)
    crosses = c >= shards - (req_devs - 1)
    blk_dev = cache.shape[0]
    slots = payload.shape[1]
    half_width = cache.shape[3] // HALVES
    slot_len = payload.shape[2]

    def remote(src, dst, send, recv, to):
        return pltpu.make_async_remote_copy(
            src_ref=src, dst_ref=dst, send_sem=send, recv_sem=recv,
            device_id=to, device_id_type=pl.DeviceIdType.MESH,
        )

    def plane_peer(step):
        return (z, lax.rem(c + step, shards))

    def line_peer(step):
        return (lax.rem(z + step, planes), c)

    barrier = pltpu.get_barrier_semaphore()
    for step in range(1, shards):
        pl.semaphore_signal(barrier, inc=1, device_id=plane_peer(step), device_id_type=pl.DeviceIdType.MESH)
    for step in range(1, planes):
        pl.semaphore_signal(barrier, inc=1, device_id=line_peer(step), device_id_type=pl.DeviceIdType.MESH)
    pl.semaphore_wait(barrier, shards + planes - 2)

    hop = remote(own, relay, hop_sem.at[0], hop_sem.at[1], line_peer(1))
    pl.when(crosses)(hop.start)
    pushes = []
    for step in range(1, req_devs):
        push = remote(own, earlier.at[place], kv_send.at[step - 1], kv_recv.at[place], plane_peer(step))
        sends = jnp.logical_and(place + step < req_devs, c + step < shards)
        pl.when(sends)(push.start)
        pushes.append((sends, push))

    gathers = []
    for half in range(HALVES):
        lanes = pl.ds(half * half_width, half_width)
        for step in range(1, planes):
            copy = remote(
                cache.at[:, :, :, lanes], column[half].at[pl.ds(z * blk_dev, blk_dev)],
                gather_send.at[half, step - 1], gather_recv.at[half, step - 1], line_peer(step),
            )
            copy.start()
            gathers.append(copy)
    for half in range(HALVES):
        column[half][pl.ds(z * blk_dev, blk_dev)] = cache[:, :, :, half * half_width : (half + 1) * half_width]

    own_block(own, q_ref, top, acc)

    def absorb_earlier(step, carry):
        slot = jnp.where(c == 0, step, place - 1 - step)
        remote(earlier.at[slot], earlier.at[slot], kv_send.at[0], kv_recv.at[slot], plane_peer(1)).wait_recv()
        earlier_block(earlier.at[slot], q_ref, top, acc)
        return carry

    def send_listed(half):
        for step in range(1, planes):
            gathers[half * (planes - 1) + step - 1].wait_recv()
        copies = []
        for step in range(shards):
            to = lax.rem(c + step, shards)
            slot = 0 if step == 0 else (step - 1) % slots
            if step > slots:
                copies[step - slots - 1].wait_send()
            target = received[half].at[pl.ds(c * capacity, capacity)]
            for i in range(capacity):
                block = column[half][wanted[to * capacity + i]]
                if step == 0:
                    received[half][c * capacity + i] = block
                else:
                    payload[half, slot, i] = block
            if step > 0:
                copy = remote(
                    payload.at[half, slot], target, list_send.at[half, slot],
                    list_recv.at[half, step - 1], plane_peer(step),
                )
                copy.start()
                copies.append(copy)
        return copies

    first = jnp.minimum(place, 1)
    later = jnp.minimum(place, req_devs - 3)
    lax.fori_loop(0, first, absorb_earlier, 0)
    forward = remote(relay, earlier.at[place], fwd_send, kv_recv.at[place], (z, 0))

    @pl.when(crosses)
    def _():
        hop.wait_recv()
        forward.start()

    lax.fori_loop(first, later, absorb_earlier, 0)
    lists = [send_listed(0)]
    lax.fori_loop(later, place, absorb_earlier, 0)
    for half in range(1, HALVES):
        lists.append(send_listed(half))
    for half in range(HALVES):
        for copy in lists[half]:
            copy.wait_recv()
        branch_blocks(half, position, count, received[half], q_ref, top, acc)
    store_result(o_ref, acc)

    pl.when(crosses)(hop.wait_send)
    pl.when(crosses)(forward.wait_send)
    for sends, push in pushes:
        pl.when(sends)(push.wait_send)
    for copy in gathers:
        copy.wait_send()
    for copies in lists:
        for copy in copies[-slots:]:
            copy.wait_send()


def local(summary_q, summary_kv, kv_cache, block_slot, tile_blocks, tile_count):
    planes, shards = lax.axis_size("branch"), lax.axis_size("ctx")
    tile_num, list_len = tile_blocks.shape
    blk_dev = kv_cache.shape[0]
    block_len = kv_cache.shape[2]
    kv_width = kv_cache.shape[3]
    groups = kv_width // HEAD
    rows = summary_q.shape[0]
    tile_rows = rows // tile_num
    repeat = summary_q.shape[1] // kv_width
    col_cap = max(2, -(-(tile_num * list_len) // shards))
    req_devs = REQ_TILES // tile_num
    entries = tile_blocks.reshape(-1)
    live_mask = (jnp.arange(list_len, dtype=jnp.int32)[None, :] < tile_count[:, None]).reshape(-1)
    block_ids = jnp.arange(block_slot.shape[0], dtype=jnp.int32)
    stored_at = jnp.sum(
        jnp.where(entries[:, None] == block_ids[None, :], block_slot[None, :], 0), axis=1
    )
    owner_dev = stored_at // blk_dev
    local_slot = stored_at % blk_dev
    requests, position = request_table(
        owner_dev % shards, live_mask, shards, col_cap, owner_dev // shards * blk_dev + local_slot
    )
    wanted = jnp.maximum(lax.all_to_all(requests, "ctx", split_axis=0, concat_axis=0, tiled=True), 0)
    position = jnp.where(live_mask, position, 0)
    own = summary_kv.reshape(rows, 2 * kv_width)
    half_width = kv_width // HALVES
    slots = min(shards - 1, STAGES)
    state = (groups, tile_num, repeat * tile_rows)
    vmem, smem = pl.BlockSpec(memory_space=pltpu.VMEM), pl.BlockSpec(memory_space=pltpu.SMEM)
    dma = pltpu.SemaphoreType.DMA
    return pl.pallas_call(
        functools.partial(join, planes, shards, col_cap),
        out_shape=jax.ShapeDtypeStruct(summary_q.shape, jnp.bfloat16),
        in_specs=[smem] * 3 + [vmem] * 3,
        out_specs=vmem,
        scratch_shapes=[
            pltpu.VMEM((req_devs - 1, rows, 2 * kv_width), jnp.bfloat16),
            pltpu.VMEM((rows, 2 * kv_width), jnp.bfloat16),
            (pltpu.VMEM((planes * blk_dev, 2, block_len, half_width), jnp.bfloat16),) * HALVES,
            pltpu.VMEM((HALVES, slots, col_cap, 2, block_len, half_width), jnp.bfloat16),
            (pltpu.VMEM((shards * col_cap, 2, block_len, half_width), jnp.bfloat16),) * HALVES,
            pltpu.VMEM(state + (HEAD,), jnp.float32),
            pltpu.VMEM(state + (2 * HEAD,), jnp.float32),
            dma((req_devs - 1,)),
            dma((req_devs - 1,)),
            dma((2,)),
            dma,
            dma((HALVES, planes - 1)),
            dma((HALVES, planes - 1)),
            dma((HALVES, slots)),
            dma((HALVES, shards - 1)),
        ],
        compiler_params=pltpu.CompilerParams(
            collective_id=0, has_side_effects=True, vmem_limit_bytes=62 * 2**20
        ),
    )(wanted.reshape(-1), position, tile_count, summary_q, own, kv_cache)


def solution(mesh):
    in_specs = (
        P(("branch", "ctx"), None),
        P(("branch", "ctx"), None, None),
        P(("branch", "ctx"), None, None, None),
        P(),
        P(("branch", "ctx"), None),
        P(("branch", "ctx")),
    )
    out_specs = P(("branch", "ctx"), None)
    return jax.shard_map(local, mesh=mesh, in_specs=in_specs, out_specs=out_specs, check_vma=False)
```

```python
import functools
import math

import jax
import jax.numpy as jnp
from jax import lax
from jax.experimental import pallas as pl
from jax.experimental.pallas import tpu as pltpu
from jax.sharding import PartitionSpec as P

HEAD = 128
REQ_TILES = 32
CHUNK = 4
HALVES = 2
STAGES = 7
SCALE = math.log2(math.e) * HEAD**-0.5


def request_table(dest_index, live_mask, count_dest, capacity, payload):
    onehot = (
        (dest_index[:, None] == jnp.arange(count_dest, dtype=jnp.int32)[None, :])
        & live_mask[:, None]
    ).astype(jnp.int32)
    rank_within = jnp.sum(onehot * (jnp.cumsum(onehot, axis=0) - 1), axis=1)
    position = dest_index * capacity + rank_within
    target = jnp.where(live_mask, position, -1)
    slot_ids = jnp.arange(count_dest * capacity, dtype=jnp.int32)
    requests = jnp.max(
        jnp.where(target[:, None] == slot_ids[None, :], payload[:, None], -1), axis=0
    )
    return (requests.reshape(count_dest, capacity), position)


def absorb(group, tile, key_rows, value_rows, mask, first, q_ref, top, acc):
    groups, tile_num = acc.shape[:2]
    tile_rows = q_ref.shape[0] // tile_num
    repeat = q_ref.shape[1] // (groups * HEAD)
    token = pl.ds(pl.multiple_of(tile * tile_rows, tile_rows), tile_rows)
    index = (group, tile)
    queries = jnp.concatenate(
        [q_ref[token, head_lanes(group * repeat + r)] for r in range(repeat)], axis=0
    )
    scores = lax.dot_general(
        queries, key_rows, (((1,), (1,)), ((), ())), preferred_element_type=jnp.float32
    )
    if mask is not None:
        scores = jnp.where(mask, scores, -jnp.inf)
    block_max = jnp.max(scores, axis=1, keepdims=True)
    ones = jnp.ones_like(value_rows)
    values = jnp.concatenate([value_rows, ones], axis=1)
    if first:
        new_max = jnp.broadcast_to(block_max, top.shape[2:])
        weights = jnp.exp2((scores - block_max) * SCALE).astype(jnp.bfloat16)
        acc[index] = jnp.dot(weights, values, preferred_element_type=jnp.float32)
    else:
        old_max = top[index]
        new_max = jnp.maximum(old_max, block_max)
        wide = jnp.concatenate([new_max] * (scores.shape[1] // HEAD), axis=1)
        weights = jnp.exp2((scores - wide) * SCALE).astype(jnp.bfloat16)
        rescale = jnp.exp2((old_max - new_max) * SCALE)
        acc[index] = acc[index] * jnp.concatenate([rescale, rescale], axis=1) + jnp.dot(
            weights, values, preferred_element_type=jnp.float32
        )
    top[index] = new_max


def head_lanes(group):
    return pl.ds(pl.multiple_of(group * HEAD, HEAD), HEAD)


def own_block(own, q_ref, top, acc):
    groups, tile_num = acc.shape[:2]
    tile_rows = own.shape[0] // tile_num
    shape = (acc.shape[2], own.shape[0])
    query_row = lax.rem(lax.broadcasted_iota(jnp.int32, shape, 0), tile_rows)
    key_row = lax.broadcasted_iota(jnp.int32, shape, 1)

    def body(group, carry):
        keys, values = own[:, head_lanes(group)], own[:, head_lanes(groups + group)]
        for tile in range(tile_num):
            mask = key_row <= query_row + tile * tile_rows
            absorb(group, tile, keys, values, mask, True, q_ref, top, acc)
        return carry

    lax.fori_loop(0, groups, body, 0)


def earlier_block(block, q_ref, top, acc):
    groups, tile_num = acc.shape[:2]

    def body(group, carry):
        keys, values = block[:, head_lanes(group)], block[:, head_lanes(groups + group)]
        for tile in range(tile_num):
            absorb(group, tile, keys, values, None, False, q_ref, top, acc)
        return carry

    lax.fori_loop(0, groups, body, 0)


def branch_blocks(half, position, count, received, q_ref, top, acc):
    groups, tile_num = acc.shape[:2]
    list_len = position.shape[0] // tile_num
    block_len = received.shape[2]
    shape = (acc.shape[2], CHUNK * block_len)
    key_block = lax.div(lax.broadcasted_iota(jnp.int32, shape, 1), block_len)

    def body(tile, carry):
        for start in range(0, list_len, CHUNK):
            where = [position[tile * list_len + start + i] for i in range(CHUNK)]
            mask = key_block < count[tile] - start
            for sub in range(groups // HALVES):
                lanes = slice(sub * HEAD, (sub + 1) * HEAD)
                keys = jnp.concatenate([received[w, 0, :, lanes] for w in where], axis=0)
                values = jnp.concatenate([received[w, 1, :, lanes] for w in where], axis=0)
                group = half * (groups // HALVES) + sub
                absorb(group, tile, keys, values, mask, False, q_ref, top, acc)
        return carry

    lax.fori_loop(0, tile_num, body, 0)


def store_result(o_ref, acc):
    groups, tile_num, stacked, _ = acc.shape
    tile_rows = o_ref.shape[0] // tile_num
    repeat = stacked // tile_rows

    def body(group, carry):
        for tile in range(tile_num):
            for r in range(repeat):
                part = acc[group, tile, r * tile_rows : (r + 1) * tile_rows, :]
                o_ref[
                    tile * tile_rows : (tile + 1) * tile_rows, head_lanes(group * repeat + r)
                ] = (part[:, :HEAD] / part[:, HEAD:]).astype(o_ref.dtype)
        return carry

    lax.fori_loop(0, groups, body, 0)


def join(
    planes, shards, capacity,
    position, count, requests, q_ref, own, cache, o_ref,
    earlier, relay, column, payload, received, top, acc, arrived, wanted,
    kv_send, kv_recv, side_send, hop_sem, fwd_send, gather_send, gather_recv, list_send, list_recv,
    ask_send, ask_recv, ask_local,
):
    z, c = lax.axis_index("branch"), lax.axis_index("ctx")
    req_devs = earlier.shape[0] + 1
    place = lax.rem(c + req_devs - 1, req_devs)
    crosses = c >= shards - (req_devs - 1)
    blk_dev = cache.shape[0]
    slots = payload.shape[1]
    half_width = cache.shape[3] // HALVES
    slot_len = payload.shape[2]

    def remote(src, dst, send, recv, to):
        return pltpu.make_async_remote_copy(
            src_ref=src, dst_ref=dst, send_sem=send, recv_sem=recv,
            device_id=to, device_id_type=pl.DeviceIdType.MESH,
        )

    def plane_peer(step):
        return (z, lax.rem(c + step, shards))

    def line_peer(step):
        return (lax.rem(z + step, planes), c)

    barrier = pltpu.get_barrier_semaphore()
    for step in range(1, shards):
        pl.semaphore_signal(barrier, inc=1, device_id=plane_peer(step), device_id_type=pl.DeviceIdType.MESH)
    for step in range(1, planes):
        pl.semaphore_signal(barrier, inc=1, device_id=line_peer(step), device_id_type=pl.DeviceIdType.MESH)
    pl.semaphore_wait(barrier, shards + planes - 2)

    asks = []
    for step in range(1, shards):
        ask = remote(
            requests.at[lax.rem(c + step, shards)], arrived.at[c],
            ask_send.at[step - 1], ask_recv.at[step - 1], plane_peer(step),
        )
        ask.start()
        asks.append(ask)
    hop = remote(own, relay, hop_sem.at[0], hop_sem.at[1], line_peer(1))
    pl.when(crosses)(hop.start)
    pushes = []
    for step in range(1, req_devs):
        push = remote(own, earlier.at[place], kv_send.at[step - 1], kv_recv.at[place], plane_peer(step))
        sends = jnp.logical_and(place + step < req_devs, c + step < shards)
        if step % 2:
            direct = place + step == req_devs - 1
            if step == 1:
                direct = jnp.logical_or(direct, lax.rem(c, 2) == 0)
            sends = jnp.logical_and(sends, direct)
        pl.when(sends)(push.start)
        pushes.append((sends, push))

    gathers = []
    for half in range(HALVES):
        lanes = pl.ds(half * half_width, half_width)
        for step in range(1, planes):
            copy = remote(
                cache.at[:, :, :, lanes], column[half].at[pl.ds(z * blk_dev, blk_dev)],
                gather_send.at[half, step - 1], gather_recv.at[half, step - 1], line_peer(step),
            )
            if half == 0:
                copy.start()
            gathers.append(copy)
    for half in range(HALVES):
        column[half][pl.ds(z * blk_dev, blk_dev)] = cache[:, :, :, half * half_width : (half + 1) * half_width]

    own_block(own, q_ref, top, acc)

    odd = lax.rem(c, 2)
    last = place == req_devs - 1
    sibling = (z, c + 1 - 2 * odd)
    near = lax.div(place, 2)

    def hand_on(slot):
        return remote(earlier.at[slot], earlier.at[slot], side_send.at[slot], kv_recv.at[slot], sibling)

    def absorb_earlier(step, carry):
        k = step - odd
        handed = place - 1 - odd * 2 - 2 * (k - near)
        slot = jnp.where(k < near, place - 2 - 2 * k, handed)
        slot = jnp.where(k < 0, place - 1, slot)
        slot = jnp.where(last, step, slot)
        copy = hand_on(slot)
        copy.wait_recv()
        straight = jnp.logical_and(jnp.logical_and(k >= 0, k < near), place < req_devs - 1)
        pl.when(straight)(copy.start)
        earlier_block(earlier.at[slot], q_ref, top, acc)
        return carry

    def ask_own():
        for ask in asks:
            ask.wait_recv()
        arrived[c] = requests[c]
        copy = pltpu.make_async_copy(arrived, wanted, ask_local)
        copy.start()
        copy.wait()

    def send_listed(half):
        for step in range(1, planes):
            gathers[half * (planes - 1) + step - 1].wait_recv()
        copies = []
        for step in range(shards):
            to = lax.rem(c + step, shards)
            slot = 0 if step == 0 else (step - 1) % slots
            if step > slots:
                copies[step - slots - 1].wait_send()
            target = received[half].at[pl.ds(c * capacity, capacity)]
            for i in range(capacity):
                block = column[half][wanted[to, 0, i]]
                if step == 0:
                    received[half][c * capacity + i] = block
                else:
                    payload[half, slot, i] = block
            if step > 0:
                copy = remote(
                    payload.at[half, slot], target, list_send.at[half, slot],
                    list_recv.at[half, step - 1], plane_peer(step),
                )
                copy.start()
                copies.append(copy)
        return copies

    marks = [jnp.minimum(place, n) for n in (1, req_devs - 4, req_devs - 3, req_devs - 2)]
    lax.fori_loop(0, marks[0], absorb_earlier, 0)
    forward = remote(relay, earlier.at[place], fwd_send, kv_recv.at[place], (z, 0))

    @pl.when(crosses)
    def _():
        hop.wait_recv()
        forward.start()

    lax.fori_loop(marks[0], marks[1], absorb_earlier, 0)
    for copy in gathers[: planes - 1]:
        copy.wait_send()
    for copy in gathers[planes - 1 :]:
        copy.start()
    ask_own()
    lax.fori_loop(marks[1], marks[2], absorb_earlier, 0)
    lists = [send_listed(0)]
    lax.fori_loop(marks[2], marks[3], absorb_earlier, 0)
    for half in range(1, HALVES):
        lists.append(send_listed(half))
    lax.fori_loop(marks[3], place, absorb_earlier, 0)
    for half in range(HALVES):
        for copy in lists[half]:
            copy.wait_recv()
        branch_blocks(half, position, count, received[half], q_ref, top, acc)
    store_result(o_ref, acc)

    pl.when(crosses)(hop.wait_send)
    pl.when(crosses)(forward.wait_send)
    for sends, push in pushes:
        pl.when(sends)(push.wait_send)
    for slot in range(req_devs - 1):
        handed = jnp.logical_and(slot < place, lax.rem(place - slot, 2) == 0)
        pl.when(jnp.logical_and(handed, place < req_devs - 1))(hand_on(slot).wait_send)
    for copy in gathers[planes - 1 :] + asks:
        copy.wait_send()
    for copies in lists:
        for copy in copies[-slots:]:
            copy.wait_send()


def local(summary_q, summary_kv, kv_cache, block_slot, tile_blocks, tile_count):
    planes, shards = lax.axis_size("branch"), lax.axis_size("ctx")
    tile_num, list_len = tile_blocks.shape
    blk_dev = kv_cache.shape[0]
    block_len = kv_cache.shape[2]
    kv_width = kv_cache.shape[3]
    groups = kv_width // HEAD
    rows = summary_q.shape[0]
    tile_rows = rows // tile_num
    repeat = summary_q.shape[1] // kv_width
    col_cap = max(2, -(-(tile_num * list_len) // shards))
    req_devs = REQ_TILES // tile_num
    entries = tile_blocks.reshape(-1)
    live_mask = (jnp.arange(list_len, dtype=jnp.int32)[None, :] < tile_count[:, None]).reshape(-1)
    block_ids = jnp.arange(block_slot.shape[0], dtype=jnp.int32)
    stored_at = jnp.sum(
        jnp.where(entries[:, None] == block_ids[None, :], block_slot[None, :], 0), axis=1
    )
    owner_dev = stored_at // blk_dev
    local_slot = stored_at % blk_dev
    requests, position = request_table(
        owner_dev % shards, live_mask, shards, col_cap, owner_dev // shards * blk_dev + local_slot
    )
    requests = jnp.pad(jnp.maximum(requests, 0), ((0, 0), (0, HEAD - col_cap)))
    requests = jnp.broadcast_to(requests[:, None, :], (shards, 8, HEAD))
    position = jnp.where(live_mask, position, 0)
    own = summary_kv.reshape(rows, 2 * kv_width)
    half_width = kv_width // HALVES
    slots = min(shards - 1, STAGES)
    state = (groups, tile_num, repeat * tile_rows)
    vmem, smem = pl.BlockSpec(memory_space=pltpu.VMEM), pl.BlockSpec(memory_space=pltpu.SMEM)
    dma = pltpu.SemaphoreType.DMA
    return pl.pallas_call(
        functools.partial(join, planes, shards, col_cap),
        out_shape=jax.ShapeDtypeStruct(summary_q.shape, jnp.bfloat16),
        in_specs=[smem] * 2 + [vmem] * 4,
        out_specs=vmem,
        scratch_shapes=[
            pltpu.VMEM((req_devs - 1, rows, 2 * kv_width), jnp.bfloat16),
            pltpu.VMEM((rows, 2 * kv_width), jnp.bfloat16),
            (pltpu.VMEM((planes * blk_dev, 2, block_len, half_width), jnp.bfloat16),) * HALVES,
            pltpu.VMEM((HALVES, slots, col_cap, 2, block_len, half_width), jnp.bfloat16),
            (pltpu.VMEM((shards * col_cap, 2, block_len, half_width), jnp.bfloat16),) * HALVES,
            pltpu.VMEM(state + (HEAD,), jnp.float32),
            pltpu.VMEM(state + (2 * HEAD,), jnp.float32),
            pltpu.VMEM((shards, 8, HEAD), jnp.int32),
            pltpu.SMEM((shards, 8, HEAD), jnp.int32),
            dma((req_devs - 1,)),
            dma((req_devs - 1,)),
            dma((req_devs - 1,)),
            dma((2,)),
            dma,
            dma((HALVES, planes - 1)),
            dma((HALVES, planes - 1)),
            dma((HALVES, slots)),
            dma((HALVES, shards - 1)),
            dma((shards - 1,)),
            dma((shards - 1,)),
            dma,
        ],
        compiler_params=pltpu.CompilerParams(
            collective_id=0, has_side_effects=True, vmem_limit_bytes=62 * 2**20
        ),
    )(position, tile_count, requests, summary_q, own, kv_cache)


def solution(mesh):
    in_specs = (
        P(("branch", "ctx"), None),
        P(("branch", "ctx"), None, None),
        P(("branch", "ctx"), None, None, None),
        P(),
        P(("branch", "ctx"), None),
        P(("branch", "ctx")),
    )
    out_specs = P(("branch", "ctx"), None)
    return jax.shard_map(local, mesh=mesh, in_specs=in_specs, out_specs=out_specs, check_vma=False)
```

```python
import functools
import math

import jax
import jax.numpy as jnp
from jax import lax
from jax.experimental import pallas as pl
from jax.experimental.pallas import tpu as pltpu
from jax.sharding import PartitionSpec as P

HEAD = 128
REQ_TILES = 32
CHUNK = 4
HALVES = 2
STAGES = 7
SCALE = math.log2(math.e) * HEAD**-0.5


def request_table(dest_index, live_mask, count_dest, capacity, payload):
    onehot = (
        (dest_index[:, None] == jnp.arange(count_dest, dtype=jnp.int32)[None, :])
        & live_mask[:, None]
    ).astype(jnp.int32)
    rank_within = jnp.sum(onehot * (jnp.cumsum(onehot, axis=0) - 1), axis=1)
    position = dest_index * capacity + rank_within
    target = jnp.where(live_mask, position, -1)
    slot_ids = jnp.arange(count_dest * capacity, dtype=jnp.int32)
    requests = jnp.max(
        jnp.where(target[:, None] == slot_ids[None, :], payload[:, None], -1), axis=0
    )
    return (requests.reshape(count_dest, capacity), position)


def absorb(group, tile, key_rows, value_rows, mask, first, q_ref, top, acc):
    groups, tile_num = acc.shape[:2]
    tile_rows = q_ref.shape[0] // tile_num
    repeat = q_ref.shape[1] // (groups * HEAD)
    token = pl.ds(pl.multiple_of(tile * tile_rows, tile_rows), tile_rows)
    index = (group, tile)
    queries = jnp.concatenate(
        [q_ref[token, head_lanes(group * repeat + r)] for r in range(repeat)], axis=0
    )
    scores = lax.dot_general(
        queries, key_rows, (((1,), (1,)), ((), ())), preferred_element_type=jnp.float32
    )
    if mask is not None:
        scores = jnp.where(mask, scores, -jnp.inf)
    block_max = jnp.max(scores, axis=1, keepdims=True)
    ones = jnp.ones_like(value_rows)
    values = jnp.concatenate([value_rows, ones], axis=1)
    if first:
        new_max = jnp.broadcast_to(block_max, top.shape[2:])
        weights = jnp.exp2((scores - block_max) * SCALE).astype(jnp.bfloat16)
        acc[index] = jnp.dot(weights, values, preferred_element_type=jnp.float32)
    else:
        old_max = top[index]
        new_max = jnp.maximum(old_max, block_max)
        wide = jnp.concatenate([new_max] * (scores.shape[1] // HEAD), axis=1)
        weights = jnp.exp2((scores - wide) * SCALE).astype(jnp.bfloat16)
        rescale = jnp.exp2((old_max - new_max) * SCALE)
        acc[index] = acc[index] * jnp.concatenate([rescale, rescale], axis=1) + jnp.dot(
            weights, values, preferred_element_type=jnp.float32
        )
    top[index] = new_max


def head_lanes(group):
    return pl.ds(pl.multiple_of(group * HEAD, HEAD), HEAD)


def own_block(own, q_ref, top, acc):
    groups, tile_num = acc.shape[:2]
    tile_rows = own.shape[0] // tile_num

    def body(group, carry):
        keys, values = own[:, head_lanes(group)], own[:, head_lanes(groups + group)]
        for tile in range(tile_num):
            seen = (tile + 1) * tile_rows
            shape = (acc.shape[2], seen)
            query_row = lax.rem(lax.broadcasted_iota(jnp.int32, shape, 0), tile_rows)
            key_row = lax.broadcasted_iota(jnp.int32, shape, 1)
            mask = key_row <= query_row + tile * tile_rows
            absorb(group, tile, keys[:seen], values[:seen], mask, True, q_ref, top, acc)
        return carry

    lax.fori_loop(0, groups, body, 0)


def earlier_block(block, q_ref, top, acc):
    groups, tile_num = acc.shape[:2]

    def body(group, carry):
        keys, values = block[:, head_lanes(group)], block[:, head_lanes(groups + group)]
        for tile in range(tile_num):
            absorb(group, tile, keys, values, None, False, q_ref, top, acc)
        return carry

    lax.fori_loop(0, groups, body, 0)


def branch_blocks(half, position, count, received, q_ref, top, acc):
    groups, tile_num = acc.shape[:2]
    list_len = position.shape[0] // tile_num
    block_len = received.shape[2]
    shape = (acc.shape[2], CHUNK * block_len)
    key_block = lax.div(lax.broadcasted_iota(jnp.int32, shape, 1), block_len)

    def body(tile, carry):
        for start in range(0, list_len, CHUNK):
            where = [position[tile * list_len + start + i] for i in range(CHUNK)]
            mask = key_block < count[tile] - start
            for sub in range(groups // HALVES):
                lanes = slice(sub * HEAD, (sub + 1) * HEAD)
                keys = jnp.concatenate([received[w, 0, :, lanes] for w in where], axis=0)
                values = jnp.concatenate([received[w, 1, :, lanes] for w in where], axis=0)
                group = half * (groups // HALVES) + sub
                absorb(group, tile, keys, values, mask, False, q_ref, top, acc)
        return carry

    lax.fori_loop(0, tile_num, body, 0)


def store_result(o_ref, acc):
    groups, tile_num, stacked, _ = acc.shape
    tile_rows = o_ref.shape[0] // tile_num
    repeat = stacked // tile_rows

    def body(group, carry):
        for tile in range(tile_num):
            for r in range(repeat):
                part = acc[group, tile, r * tile_rows : (r + 1) * tile_rows, :]
                o_ref[
                    tile * tile_rows : (tile + 1) * tile_rows, head_lanes(group * repeat + r)
                ] = (part[:, :HEAD] / part[:, HEAD:]).astype(o_ref.dtype)
        return carry

    lax.fori_loop(0, groups, body, 0)


def join(
    planes, shards, capacity,
    position, count, requests, q_ref, own, cache, o_ref,
    earlier, relay, column, payload, received, top, acc, arrived, wanted,
    kv_send, kv_recv, side_send, hop_sem, fwd_send, gather_send, gather_recv, list_send, list_recv,
    ask_send, ask_recv, ask_local,
):
    z, c = lax.axis_index("branch"), lax.axis_index("ctx")
    req_devs = earlier.shape[0] + 1
    place = lax.rem(c + req_devs - 1, req_devs)
    crosses = c >= shards - (req_devs - 1)
    blk_dev = cache.shape[0]
    slots = payload.shape[1]
    half_width = cache.shape[3] // HALVES
    slot_len = payload.shape[2]

    def remote(src, dst, send, recv, to):
        return pltpu.make_async_remote_copy(
            src_ref=src, dst_ref=dst, send_sem=send, recv_sem=recv,
            device_id=to, device_id_type=pl.DeviceIdType.MESH,
        )

    def plane_peer(step):
        return (z, lax.rem(c + step, shards))

    def line_peer(step):
        return (lax.rem(z + step, planes), c)

    barrier = pltpu.get_barrier_semaphore()
    for step in range(1, shards):
        pl.semaphore_signal(barrier, inc=1, device_id=plane_peer(step), device_id_type=pl.DeviceIdType.MESH)
    for step in range(1, planes):
        pl.semaphore_signal(barrier, inc=1, device_id=line_peer(step), device_id_type=pl.DeviceIdType.MESH)
    pl.semaphore_wait(barrier, shards + planes - 2)

    asks = []
    for step in range(1, shards):
        ask = remote(
            requests.at[lax.rem(c + step, shards)], arrived.at[c],
            ask_send.at[step - 1], ask_recv.at[step - 1], plane_peer(step),
        )
        ask.start()
        asks.append(ask)
    hop = remote(own, relay, hop_sem.at[0], hop_sem.at[1], line_peer(1))
    pl.when(crosses)(hop.start)
    pushes = []
    for step in range(1, req_devs):
        push = remote(own, earlier.at[place], kv_send.at[step - 1], kv_recv.at[place], plane_peer(step))
        sends = jnp.logical_and(place + step < req_devs, c + step < shards)
        if step % 2:
            direct = place + step == req_devs - 1
            if step == 1:
                direct = jnp.logical_or(direct, lax.rem(c, 2) == 0)
            sends = jnp.logical_and(sends, direct)
        pl.when(sends)(push.start)
        pushes.append((sends, push))

    gathers = []
    for half in range(HALVES):
        lanes = pl.ds(half * half_width, half_width)
        for step in range(1, planes):
            copy = remote(
                cache.at[:, :, :, lanes], column[half].at[pl.ds(z * blk_dev, blk_dev)],
                gather_send.at[half, step - 1], gather_recv.at[half, step - 1], line_peer(step),
            )
            copy.start()
            gathers.append(copy)
    for half in range(HALVES):
        column[half][pl.ds(z * blk_dev, blk_dev)] = cache[:, :, :, half * half_width : (half + 1) * half_width]

    own_block(own, q_ref, top, acc)

    odd = lax.rem(c, 2)
    last = place == req_devs - 1
    sibling = (z, c + 1 - 2 * odd)
    near = lax.div(place, 2)

    def hand_on(slot):
        return remote(earlier.at[slot], earlier.at[slot], side_send.at[slot], kv_recv.at[slot], sibling)

    def absorb_earlier(step, carry):
        k = step - odd
        handed = place - 1 - odd * 2 - 2 * (k - near)
        slot = jnp.where(k < near, place - 2 - 2 * k, handed)
        slot = jnp.where(k < 0, place - 1, slot)
        slot = jnp.where(last, step, slot)
        copy = hand_on(slot)
        copy.wait_recv()
        straight = jnp.logical_and(jnp.logical_and(k >= 0, k < near), place < req_devs - 1)
        pl.when(straight)(copy.start)
        earlier_block(earlier.at[slot], q_ref, top, acc)
        return carry

    def ask_own():
        for ask in asks:
            ask.wait_recv()
        arrived[c] = requests[c]
        copy = pltpu.make_async_copy(arrived, wanted, ask_local)
        copy.start()
        copy.wait()

    def send_listed(half):
        for step in range(1, planes):
            gathers[half * (planes - 1) + step - 1].wait_recv()
        copies = []
        for step in range(shards):
            to = lax.rem(c + step, shards)
            slot = 0 if step == 0 else (step - 1) % slots
            if step > slots:
                copies[step - slots - 1].wait_send()
            target = received[half].at[pl.ds(c * capacity, capacity)]
            for i in range(capacity):
                block = column[half][wanted[to, 0, i]]
                if step == 0:
                    received[half][c * capacity + i] = block
                else:
                    payload[half, slot, i] = block
            if step > 0:
                copy = remote(
                    payload.at[half, slot], target, list_send.at[half, slot],
                    list_recv.at[half, step - 1], plane_peer(step),
                )
                copy.start()
                copies.append(copy)
        return copies

    marks = [jnp.minimum(place, n) for n in (1, req_devs - 5, req_devs - 3)]
    lax.fori_loop(0, marks[0], absorb_earlier, 0)
    forward = remote(relay, earlier.at[place], fwd_send, kv_recv.at[place], (z, 0))

    @pl.when(crosses)
    def _():
        hop.wait_recv()
        forward.start()

    lax.fori_loop(marks[0], marks[1], absorb_earlier, 0)
    ask_own()
    lists = [send_listed(0)]
    lax.fori_loop(marks[1], marks[2], absorb_earlier, 0)
    lists.append(send_listed(1))

    def absorb_listed(half):
        for copy in lists[half]:
            copy.wait_recv()
        branch_blocks(half, position, count, received[half], q_ref, top, acc)

    absorb_listed(0)
    lax.fori_loop(marks[2], place, absorb_earlier, 0)
    absorb_listed(1)
    store_result(o_ref, acc)

    pl.when(crosses)(hop.wait_send)
    pl.when(crosses)(forward.wait_send)
    for sends, push in pushes:
        pl.when(sends)(push.wait_send)
    for slot in range(req_devs - 1):
        handed = jnp.logical_and(slot < place, lax.rem(place - slot, 2) == 0)
        pl.when(jnp.logical_and(handed, place < req_devs - 1))(hand_on(slot).wait_send)
    for copy in gathers + asks:
        copy.wait_send()
    for copies in lists:
        for copy in copies[-slots:]:
            copy.wait_send()


def local(summary_q, summary_kv, kv_cache, block_slot, tile_blocks, tile_count):
    planes, shards = lax.axis_size("branch"), lax.axis_size("ctx")
    tile_num, list_len = tile_blocks.shape
    blk_dev = kv_cache.shape[0]
    block_len = kv_cache.shape[2]
    kv_width = kv_cache.shape[3]
    groups = kv_width // HEAD
    rows = summary_q.shape[0]
    tile_rows = rows // tile_num
    repeat = summary_q.shape[1] // kv_width
    col_cap = max(2, -(-(tile_num * list_len) // shards))
    req_devs = REQ_TILES // tile_num
    entries = tile_blocks.reshape(-1)
    live_mask = (jnp.arange(list_len, dtype=jnp.int32)[None, :] < tile_count[:, None]).reshape(-1)
    block_ids = jnp.arange(block_slot.shape[0], dtype=jnp.int32)
    stored_at = jnp.sum(
        jnp.where(entries[:, None] == block_ids[None, :], block_slot[None, :], 0), axis=1
    )
    owner_dev = stored_at // blk_dev
    local_slot = stored_at % blk_dev
    requests, position = request_table(
        owner_dev % shards, live_mask, shards, col_cap, owner_dev // shards * blk_dev + local_slot
    )
    requests = jnp.pad(jnp.maximum(requests, 0), ((0, 0), (0, HEAD - col_cap)))
    requests = jnp.broadcast_to(requests[:, None, :], (shards, 8, HEAD))
    position = jnp.where(live_mask, position, 0)
    own = summary_kv.reshape(rows, 2 * kv_width)
    half_width = kv_width // HALVES
    slots = min(shards - 1, STAGES)
    state = (groups, tile_num, repeat * tile_rows)
    vmem, smem = pl.BlockSpec(memory_space=pltpu.VMEM), pl.BlockSpec(memory_space=pltpu.SMEM)
    dma = pltpu.SemaphoreType.DMA
    return pl.pallas_call(
        functools.partial(join, planes, shards, col_cap),
        out_shape=jax.ShapeDtypeStruct(summary_q.shape, jnp.bfloat16),
        in_specs=[smem] * 2 + [vmem] * 4,
        out_specs=vmem,
        scratch_shapes=[
            pltpu.VMEM((req_devs - 1, rows, 2 * kv_width), jnp.bfloat16),
            pltpu.VMEM((rows, 2 * kv_width), jnp.bfloat16),
            (pltpu.VMEM((planes * blk_dev, 2, block_len, half_width), jnp.bfloat16),) * HALVES,
            pltpu.VMEM((HALVES, slots, col_cap, 2, block_len, half_width), jnp.bfloat16),
            (pltpu.VMEM((shards * col_cap, 2, block_len, half_width), jnp.bfloat16),) * HALVES,
            pltpu.VMEM(state + (HEAD,), jnp.float32),
            pltpu.VMEM(state + (2 * HEAD,), jnp.float32),
            pltpu.VMEM((shards, 8, HEAD), jnp.int32),
            pltpu.SMEM((shards, 8, HEAD), jnp.int32),
            dma((req_devs - 1,)),
            dma((req_devs - 1,)),
            dma((req_devs - 1,)),
            dma((2,)),
            dma,
            dma((HALVES, planes - 1)),
            dma((HALVES, planes - 1)),
            dma((HALVES, slots)),
            dma((HALVES, shards - 1)),
            dma((shards - 1,)),
            dma((shards - 1,)),
            dma,
        ],
        compiler_params=pltpu.CompilerParams(
            collective_id=0, has_side_effects=True, vmem_limit_bytes=62 * 2**20
        ),
    )(position, tile_count, requests, summary_q, own, kv_cache)


def solution(mesh):
    in_specs = (
        P(("branch", "ctx"), None),
        P(("branch", "ctx"), None, None),
        P(("branch", "ctx"), None, None, None),
        P(),
        P(("branch", "ctx"), None),
        P(("branch", "ctx")),
    )
    out_specs = P(("branch", "ctx"), None)
    return jax.shard_map(local, mesh=mesh, in_specs=in_specs, out_specs=out_specs, check_vma=False)
```

```python
import functools
import math

import jax
import jax.numpy as jnp
from jax import lax
from jax.experimental import pallas as pl
from jax.experimental.pallas import tpu as pltpu
from jax.sharding import PartitionSpec as P

HEAD = 128
REQ_TILES = 32
CHUNK = 4
HALVES = 2
STAGES = 7
SCALE = math.log2(math.e) * HEAD**-0.5


def request_table(dest_index, live_mask, count_dest, capacity, payload):
    onehot = (
        (dest_index[:, None] == jnp.arange(count_dest, dtype=jnp.int32)[None, :])
        & live_mask[:, None]
    ).astype(jnp.int32)
    rank_within = jnp.sum(onehot * (jnp.cumsum(onehot, axis=0) - 1), axis=1)
    position = dest_index * capacity + rank_within
    target = jnp.where(live_mask, position, -1)
    slot_ids = jnp.arange(count_dest * capacity, dtype=jnp.int32)
    requests = jnp.max(
        jnp.where(target[:, None] == slot_ids[None, :], payload[:, None], -1), axis=0
    )
    return (requests.reshape(count_dest, capacity), position)


def absorb(group, tile, key_rows, value_rows, mask, first, q_ref, top, acc):
    groups, tile_num = acc.shape[:2]
    tile_rows = q_ref.shape[0] // tile_num
    repeat = q_ref.shape[1] // (groups * HEAD)
    token = pl.ds(pl.multiple_of(tile * tile_rows, tile_rows), tile_rows)
    index = (group, tile)
    queries = jnp.concatenate(
        [q_ref[token, head_lanes(group * repeat + r)] for r in range(repeat)], axis=0
    )
    scores = lax.dot_general(
        queries, key_rows, (((1,), (1,)), ((), ())), preferred_element_type=jnp.float32
    )
    if mask is not None:
        scores = jnp.where(mask, scores, -jnp.inf)
    block_max = jnp.max(scores, axis=1, keepdims=True)
    ones = jnp.ones_like(value_rows)
    values = jnp.concatenate([value_rows, ones], axis=1)
    if first:
        new_max = jnp.broadcast_to(block_max, top.shape[2:])
        weights = jnp.exp2((scores - block_max) * SCALE).astype(jnp.bfloat16)
        acc[index] = jnp.dot(weights, values, preferred_element_type=jnp.float32)
    else:
        old_max = top[index]
        new_max = jnp.maximum(old_max, block_max)
        wide = jnp.concatenate([new_max] * (scores.shape[1] // HEAD), axis=1)
        weights = jnp.exp2((scores - wide) * SCALE).astype(jnp.bfloat16)
        rescale = jnp.exp2((old_max - new_max) * SCALE)
        acc[index] = acc[index] * jnp.concatenate([rescale, rescale], axis=1) + jnp.dot(
            weights, values, preferred_element_type=jnp.float32
        )
    top[index] = new_max


def head_lanes(group):
    return pl.ds(pl.multiple_of(group * HEAD, HEAD), HEAD)


def own_block(own, q_ref, top, acc):
    groups, tile_num = acc.shape[:2]
    tile_rows = own.shape[0] // tile_num

    def body(group, carry):
        keys, values = own[:, head_lanes(group)], own[:, head_lanes(groups + group)]
        for tile in range(tile_num):
            seen = (tile + 1) * tile_rows
            shape = (acc.shape[2], seen)
            query_row = lax.rem(lax.broadcasted_iota(jnp.int32, shape, 0), tile_rows)
            key_row = lax.broadcasted_iota(jnp.int32, shape, 1)
            mask = key_row <= query_row + tile * tile_rows
            absorb(group, tile, keys[:seen], values[:seen], mask, True, q_ref, top, acc)
        return carry

    lax.fori_loop(0, groups, body, 0)


def earlier_block(block, q_ref, top, acc):
    groups, tile_num = acc.shape[:2]

    def body(group, carry):
        keys, values = block[:, head_lanes(group)], block[:, head_lanes(groups + group)]
        for tile in range(tile_num):
            absorb(group, tile, keys, values, None, False, q_ref, top, acc)
        return carry

    lax.fori_loop(0, groups, body, 0)


def branch_blocks(half, position, count, received, q_ref, top, acc):
    groups, tile_num = acc.shape[:2]
    list_len = position.shape[0] // tile_num
    block_len = received.shape[2]
    shape = (acc.shape[2], CHUNK * block_len)
    key_block = lax.div(lax.broadcasted_iota(jnp.int32, shape, 1), block_len)

    def body(tile, carry):
        for start in range(0, list_len, CHUNK):
            where = [position[tile * list_len + start + i] for i in range(CHUNK)]
            mask = key_block < count[tile] - start
            for sub in range(groups // HALVES):
                lanes = slice(sub * HEAD, (sub + 1) * HEAD)
                keys = jnp.concatenate([received[w, 0, :, lanes] for w in where], axis=0)
                values = jnp.concatenate([received[w, 1, :, lanes] for w in where], axis=0)
                group = half * (groups // HALVES) + sub
                absorb(group, tile, keys, values, mask, False, q_ref, top, acc)
        return carry

    lax.fori_loop(0, tile_num, body, 0)


def store_result(o_ref, acc):
    groups, tile_num, stacked, _ = acc.shape
    tile_rows = o_ref.shape[0] // tile_num
    repeat = stacked // tile_rows

    def body(group, carry):
        for tile in range(tile_num):
            for r in range(repeat):
                part = acc[group, tile, r * tile_rows : (r + 1) * tile_rows, :]
                o_ref[
                    tile * tile_rows : (tile + 1) * tile_rows, head_lanes(group * repeat + r)
                ] = (part[:, :HEAD] / part[:, HEAD:]).astype(o_ref.dtype)
        return carry

    lax.fori_loop(0, groups, body, 0)


def join(
    planes, shards, capacity,
    position, count, requests, q_ref, own, cache, o_ref,
    earlier, relay, column, payload, received, top, acc, arrived, wanted,
    kv_send, kv_recv, side_send, hop_sem, fwd_send, gather_send, gather_recv, list_send, list_recv,
    ask_send, ask_recv, ask_local,
):
    z, c = lax.axis_index("branch"), lax.axis_index("ctx")
    req_devs = earlier.shape[0] + 1
    place = lax.rem(c + req_devs - 1, req_devs)
    crosses = c >= shards - (req_devs - 1)
    blk_dev = cache.shape[0]
    slots = payload.shape[1]
    half_width = cache.shape[3] // HALVES
    slot_len = payload.shape[2]

    def remote(src, dst, send, recv, to):
        return pltpu.make_async_remote_copy(
            src_ref=src, dst_ref=dst, send_sem=send, recv_sem=recv,
            device_id=to, device_id_type=pl.DeviceIdType.MESH,
        )

    def plane_peer(step):
        return (z, lax.rem(c + step, shards))

    def line_peer(step):
        return (lax.rem(z + step, planes), c)

    barrier = pltpu.get_barrier_semaphore()
    for step in range(1, shards):
        pl.semaphore_signal(barrier, inc=1, device_id=plane_peer(step), device_id_type=pl.DeviceIdType.MESH)
    for step in range(1, planes):
        pl.semaphore_signal(barrier, inc=1, device_id=line_peer(step), device_id_type=pl.DeviceIdType.MESH)
    pl.semaphore_wait(barrier, shards + planes - 2)

    asks = []
    for step in range(1, shards):
        ask = remote(
            requests.at[lax.rem(c + step, shards)], arrived.at[c],
            ask_send.at[step - 1], ask_recv.at[step - 1], plane_peer(step),
        )
        ask.start()
        asks.append(ask)
    hop = remote(own, relay, hop_sem.at[0], hop_sem.at[1], line_peer(1))
    pl.when(crosses)(hop.start)
    pushes = []
    for step in range(1, req_devs):
        push = remote(own, earlier.at[place], kv_send.at[step - 1], kv_recv.at[place], plane_peer(step))
        sends = jnp.logical_and(place + step < req_devs, c + step < shards)
        if step % 2:
            direct = place + step == req_devs - 1
            if step == 1:
                direct = jnp.logical_or(direct, lax.rem(c, 2) == 0)
            sends = jnp.logical_and(sends, direct)
        pl.when(sends)(push.start)
        pushes.append((sends, push))

    gathers = []
    for half in range(HALVES):
        lanes = pl.ds(half * half_width, half_width)
        for step in range(1, planes):
            copy = remote(
                cache.at[:, :, :, lanes], column[half].at[pl.ds(z * blk_dev, blk_dev)],
                gather_send.at[half, step - 1], gather_recv.at[half, step - 1], line_peer(step),
            )
            if half == 0:
                copy.start()
            gathers.append(copy)
    for half in range(HALVES):
        column[half][pl.ds(z * blk_dev, blk_dev)] = cache[:, :, :, half * half_width : (half + 1) * half_width]

    own_block(own, q_ref, top, acc)

    odd = lax.rem(c, 2)
    last = place == req_devs - 1
    sibling = (z, c + 1 - 2 * odd)
    near = lax.div(place, 2)

    def hand_on(slot):
        return remote(earlier.at[slot], earlier.at[slot], side_send.at[slot], kv_recv.at[slot], sibling)

    def absorb_earlier(step, carry):
        k = step - odd
        handed = place - 1 - odd * 2 - 2 * (k - near)
        slot = jnp.where(k < near, place - 2 - 2 * k, handed)
        slot = jnp.where(k < 0, place - 1, slot)
        slot = jnp.where(last, step, slot)
        copy = hand_on(slot)
        copy.wait_recv()
        straight = jnp.logical_and(jnp.logical_and(k >= 0, k < near), place < req_devs - 1)
        pl.when(straight)(copy.start)
        earlier_block(earlier.at[slot], q_ref, top, acc)
        return carry

    def ask_own():
        for ask in asks:
            ask.wait_recv()
        arrived[c] = requests[c]
        copy = pltpu.make_async_copy(arrived, wanted, ask_local)
        copy.start()
        copy.wait()

    def send_listed(half):
        for step in range(1, planes):
            gathers[half * (planes - 1) + step - 1].wait_recv()
        copies = []
        for step in range(shards):
            to = lax.rem(c + step, shards)
            slot = 0 if step == 0 else (step - 1) % slots
            if step > slots:
                copies[step - slots - 1].wait_send()
            target = received[half].at[pl.ds(c * capacity, capacity)]
            for i in range(capacity):
                block = column[half][wanted[to, 0, i]]
                if step == 0:
                    received[half][c * capacity + i] = block
                else:
                    payload[half, slot, i] = block
            if step > 0:
                copy = remote(
                    payload.at[half, slot], target, list_send.at[half, slot],
                    list_recv.at[half, step - 1], plane_peer(step),
                )
                copy.start()
                copies.append(copy)
        return copies

    marks = [jnp.minimum(place, n) for n in (1, 2, req_devs - 5, req_devs - 3)]
    lax.fori_loop(0, marks[0], absorb_earlier, 0)
    forward = remote(relay, earlier.at[place], fwd_send, kv_recv.at[place], (z, 0))

    @pl.when(crosses)
    def _():
        hop.wait_recv()
        forward.start()

    lax.fori_loop(marks[0], marks[1], absorb_earlier, 0)
    for copy in gathers[: planes - 1]:
        copy.wait_send()
    for copy in gathers[planes - 1 :]:
        copy.start()
    lax.fori_loop(marks[1], marks[2], absorb_earlier, 0)
    ask_own()
    lists = [send_listed(0)]
    lax.fori_loop(marks[2], marks[3], absorb_earlier, 0)
    lists.append(send_listed(1))

    def absorb_listed(half):
        for copy in lists[half]:
            copy.wait_recv()
        branch_blocks(half, position, count, received[half], q_ref, top, acc)

    absorb_listed(0)
    lax.fori_loop(marks[3], place, absorb_earlier, 0)
    absorb_listed(1)
    store_result(o_ref, acc)

    pl.when(crosses)(hop.wait_send)
    pl.when(crosses)(forward.wait_send)
    for sends, push in pushes:
        pl.when(sends)(push.wait_send)
    for slot in range(req_devs - 1):
        handed = jnp.logical_and(slot < place, lax.rem(place - slot, 2) == 0)
        pl.when(jnp.logical_and(handed, place < req_devs - 1))(hand_on(slot).wait_send)
    for copy in gathers[planes - 1 :] + asks:
        copy.wait_send()
    for copies in lists:
        for copy in copies[-slots:]:
            copy.wait_send()


def local(summary_q, summary_kv, kv_cache, block_slot, tile_blocks, tile_count):
    planes, shards = lax.axis_size("branch"), lax.axis_size("ctx")
    tile_num, list_len = tile_blocks.shape
    blk_dev = kv_cache.shape[0]
    block_len = kv_cache.shape[2]
    kv_width = kv_cache.shape[3]
    groups = kv_width // HEAD
    rows = summary_q.shape[0]
    tile_rows = rows // tile_num
    repeat = summary_q.shape[1] // kv_width
    col_cap = max(2, -(-(tile_num * list_len) // shards))
    req_devs = REQ_TILES // tile_num
    entries = tile_blocks.reshape(-1)
    live_mask = (jnp.arange(list_len, dtype=jnp.int32)[None, :] < tile_count[:, None]).reshape(-1)
    block_ids = jnp.arange(block_slot.shape[0], dtype=jnp.int32)
    stored_at = jnp.sum(
        jnp.where(entries[:, None] == block_ids[None, :], block_slot[None, :], 0), axis=1
    )
    owner_dev = stored_at // blk_dev
    local_slot = stored_at % blk_dev
    requests, position = request_table(
        owner_dev % shards, live_mask, shards, col_cap, owner_dev // shards * blk_dev + local_slot
    )
    requests = jnp.pad(jnp.maximum(requests, 0), ((0, 0), (0, HEAD - col_cap)))
    requests = jnp.broadcast_to(requests[:, None, :], (shards, 8, HEAD))
    position = jnp.where(live_mask, position, 0)
    own = summary_kv.reshape(rows, 2 * kv_width)
    half_width = kv_width // HALVES
    slots = min(shards - 1, STAGES)
    state = (groups, tile_num, repeat * tile_rows)
    vmem, smem = pl.BlockSpec(memory_space=pltpu.VMEM), pl.BlockSpec(memory_space=pltpu.SMEM)
    dma = pltpu.SemaphoreType.DMA
    return pl.pallas_call(
        functools.partial(join, planes, shards, col_cap),
        out_shape=jax.ShapeDtypeStruct(summary_q.shape, jnp.bfloat16),
        in_specs=[smem] * 2 + [vmem] * 4,
        out_specs=vmem,
        scratch_shapes=[
            pltpu.VMEM((req_devs - 1, rows, 2 * kv_width), jnp.bfloat16),
            pltpu.VMEM((rows, 2 * kv_width), jnp.bfloat16),
            (pltpu.VMEM((planes * blk_dev, 2, block_len, half_width), jnp.bfloat16),) * HALVES,
            pltpu.VMEM((HALVES, slots, col_cap, 2, block_len, half_width), jnp.bfloat16),
            (pltpu.VMEM((shards * col_cap, 2, block_len, half_width), jnp.bfloat16),) * HALVES,
            pltpu.VMEM(state + (HEAD,), jnp.float32),
            pltpu.VMEM(state + (2 * HEAD,), jnp.float32),
            pltpu.VMEM((shards, 8, HEAD), jnp.int32),
            pltpu.SMEM((shards, 8, HEAD), jnp.int32),
            dma((req_devs - 1,)),
            dma((req_devs - 1,)),
            dma((req_devs - 1,)),
            dma((2,)),
            dma,
            dma((HALVES, planes - 1)),
            dma((HALVES, planes - 1)),
            dma((HALVES, slots)),
            dma((HALVES, shards - 1)),
            dma((shards - 1,)),
            dma((shards - 1,)),
            dma,
        ],
        compiler_params=pltpu.CompilerParams(
            collective_id=0, has_side_effects=True, vmem_limit_bytes=62 * 2**20
        ),
    )(position, tile_count, requests, summary_q, own, kv_cache)


def solution(mesh):
    in_specs = (
        P(("branch", "ctx"), None),
        P(("branch", "ctx"), None, None),
        P(("branch", "ctx"), None, None, None),
        P(),
        P(("branch", "ctx"), None),
        P(("branch", "ctx")),
    )
    out_specs = P(("branch", "ctx"), None)
    return jax.shard_map(local, mesh=mesh, in_specs=in_specs, out_specs=out_specs, check_vma=False)
```
